32 devices in a mesh: gx: 8 (over z, x), gy: 2 (over core), gz: 2 (over y).
Axes of the slice: x: 2, y: 2, z: 4, core: 2. Of those that a mesh axis runs over, the one named last changes fastest.
Arguments:
- features: bfloat16 [8, 2, 2, 128, 512], P('gx', 'gy', 'gz'), may hold values from -6 to 6
- fraction: bfloat16 [8, 2, 2, 3, 128], P('gx', 'gy', 'gz'), may hold values from 0 to 0.98828125
- cell_index: int32 [8, 2, 2, 3, 128], P('gx', 'gy', 'gz'), may hold values from 0 to 127, as said below
- species: int32 [8, 2, 2, 128], P('gx', 'gy', 'gz'), may hold values from 0 to 1
- octant_rows: int32 [8, 2, 2, 8, 14], P('gx', 'gy', 'gz'), may hold values from 0 to 127, as said below
- neighbours: int32 [8, 2, 2, 16, 128], P('gx', 'gy', 'gz'), may hold values from 0 to 912, as said below
- radial_in: bfloat16 [2, 8, 64], replicated, may hold values from -2 to 2
- radial_out: bfloat16 [2, 64, 512], replicated, may hold values from -1.5 to 1.5
- mix_weight: bfloat16 [2, 2, 128, 128], replicated, may hold values from -0.5 to 0.5
- readout: bfloat16 [128, 2], replicated, may hold values from -0.125 to 0.125
- species_table: float32 [2, 2], replicated, may hold values from -4 to 4
Outputs:
- new_features: bfloat16 [8, 2, 2, 128, 512], P('gx', 'gy', 'gz')
- site_energy: float32 [8, 2, 2, 128], P('gx', 'gy', 'gz')
- recip_force: float32 [8, 2, 2, 3, 128], P('gx', 'gy', 'gz')
The draws below stay inside these ranges and needn't reach their ends.
Inputs may be any that keep to these rules, and one draw needn't show every extreme that they name: `cell_index`: component x lies below 32, component y below 128, component z below 128. `octant_rows`: each octant's list holds 14 different atoms of the domain. `neighbours`: entries are rows of the domain's table; 912 is an empty slot; an atom never lists itself, and the other entries of a column are different; the cell of a listed row (cell_index plus its shift) lies within 8 cells of the atom's cell.
All inputs are finite; a program needn't handle non-finite values.
Results may differ from the reference program's by a relative error of at most 0.0051.
Values may be sent and summed in bfloat16 or wider, within the bound.
A program may use at most 128 MiB of HBM per device.

```python
import math
import jax
import jax.numpy as jnp
from jax import lax

C = 128
FEAT = 512
NB = 8
HID = 64
LAYERS = 2
NEIGH = 16
NSPEC = 2
RCUT = 8
ENV = 7
MESH = 256
ATOMS = 128
GHOST = 14
NCAND = 912
BX = 32
BY = 128
BZ = 128
N_GX = 8
N_GY = 2
N_GZ = 2


def outer_cells_drawn():
    found = []
    for first in range(4):
        for second in range(4):
            for third in range(4):
                if 0 < first < 3 and 0 < second < 3 and (0 < third < 3):
                    continue
                found.append((first, second, third))
    return found


def offset_of_drawn(coord):
    return -1 if coord == 0 else 1 if coord == 3 else 0


def source_of_drawn(coord):
    return 1 if coord == 0 else 0 if coord == 3 else coord - 1


def layout(key):
    device_total = N_GX * N_GY * N_GZ
    pair_total = ATOMS // 2
    span_sizes = jnp.array([BX, BY, BZ], jnp.int32).reshape(1, 1, 1, 3, 1)
    half_sizes = span_sizes // 2
    raw_bits = jax.random.randint(jax.random.fold_in(key, 101), (N_GX, N_GY, N_GZ, 3, pair_total), 0, 1 << 24)
    lead_raw = raw_bits % half_sizes
    axis_pick = jax.random.randint(jax.random.fold_in(key, 104), (N_GX, N_GY, N_GZ, 1, pair_total), 1, 3)
    coin_flip = jax.random.randint(jax.random.fold_in(key, 105), (N_GX, N_GY, N_GZ, 1, pair_total), 0, 2)
    step_sign = jnp.where(lead_raw == half_sizes - 1, -1, jnp.where(lead_raw == 0, 1, 2 * coin_flip - 1))
    on_axis = (jnp.arange(3, dtype=jnp.int32).reshape(1, 1, 1, 3, 1) == axis_pick).astype(jnp.int32)
    partner_raw = lead_raw + step_sign * on_axis
    raw_cells = jnp.stack([lead_raw, partner_raw], axis=5).reshape(N_GX, N_GY, N_GZ, 3, ATOMS)
    pair_orders = jax.vmap(lambda subkey: jax.random.permutation(subkey, pair_total))(jax.random.split(jax.random.fold_in(key, 102), device_total))
    pair_orders = pair_orders.astype(jnp.int32).reshape(N_GX, N_GY, N_GZ, pair_total)
    orders = jnp.stack([2 * pair_orders, 2 * pair_orders + 1], axis=4).reshape(N_GX, N_GY, N_GZ, ATOMS)
    octant_of = orders // (ATOMS // 8)
    upper_half = jnp.stack([octant_of // 4, octant_of // 2 % 2, octant_of % 2], axis=3).astype(jnp.int32)
    cells = upper_half * half_sizes + raw_cells
    depth_face = jnp.where(upper_half == 1, span_sizes - 1 - cells, cells)
    nearest = jnp.min(depth_face, axis=3)
    reach_max = BX + BY + BZ
    chosen = []
    for octant in range(8):
        bit_pattern = jnp.array([octant // 4, octant // 2 % 2, octant % 2], jnp.int32).reshape(1, 1, 1, 3, 1)
        inside = jnp.all(upper_half == bit_pattern, axis=3)
        scores = jnp.where(inside, reach_max - nearest, 0) * ATOMS + orders
        chosen.append(lax.top_k(scores, GHOST)[1])
    octants = jnp.stack(chosen, axis=3).astype(jnp.int32)
    pieces = [cells]
    for corner in outer_cells_drawn():
        roll_by = (-offset_of_drawn(corner[0]), -offset_of_drawn(corner[1]), -offset_of_drawn(corner[2]))
        octant = 4 * source_of_drawn(corner[0]) + 2 * source_of_drawn(corner[1]) + source_of_drawn(corner[2])
        source_cells = jnp.roll(cells, roll_by, (0, 1, 2))
        source_rows = jnp.roll(octants[:, :, :, octant], roll_by, (0, 1, 2))
        picker = jnp.broadcast_to(source_rows[:, :, :, None, :], (N_GX, N_GY, N_GZ, 3, GHOST))
        picked = jnp.take_along_axis(source_cells, picker, axis=4)
        shifted = picked + jnp.array([offset_of_drawn(corner[0]) * BX, offset_of_drawn(corner[1]) * BY, offset_of_drawn(corner[2]) * BZ], jnp.int32).reshape(1, 1, 1, 3, 1)
        pieces.append(shifted)
    candidates = jnp.concatenate(pieces, axis=4).reshape(device_total, 3, NCAND)
    shuffles = jax.vmap(lambda subkey: jax.random.permutation(subkey, NCAND))(jax.random.split(jax.random.fold_in(key, 103), device_total)).astype(jnp.int32)
    beyond = RCUT * RCUT + 1

    def pick_slots(inputs):
        located, shuffle = inputs
        differ = located[:, :ATOMS, None] - located[:, None, :]
        distance = jnp.sum(differ * differ, axis=0)
        is_self = jnp.arange(ATOMS, dtype=jnp.int32)[:, None] == jnp.arange(NCAND, dtype=jnp.int32)[None, :]
        measure = jnp.where(is_self, beyond, jnp.minimum(distance, beyond))
        nearest_slots = lax.top_k(-(measure * NCAND + shuffle[None, :]), NEIGH)[1]
        near_value = jnp.take_along_axis(measure, nearest_slots, axis=1)
        return jnp.transpose(jnp.where(near_value <= RCUT * RCUT, nearest_slots, NCAND)).astype(jnp.int32)
    links = lax.map(pick_slots, (candidates, shuffles)).reshape(N_GX, N_GY, N_GZ, NEIGH, ATOMS)
    return (cells.astype(jnp.int32), octants, links)


def draw_cell_index(key, part):
    return layout(key)[0]


def draw_octant_rows(key, part):
    return layout(key)[1]


def draw_neighbours(key, part):
    return layout(key)[2]


def draw_species(key, part):
    leading = jax.random.randint(jax.random.fold_in(key, 201), (N_GX, N_GY, N_GZ, ATOMS // 2), 0, NSPEC)
    partner = (leading + 1) % NSPEC
    return jnp.stack([leading, partner], axis=4).reshape(N_GX, N_GY, N_GZ, ATOMS).astype(jnp.int32)


def draw_species_table(key, part):
    signs = jnp.where(jnp.arange(NSPEC, dtype=jnp.int32) % 2 == 0, 1.0, -1.0).astype(jnp.float32)
    energy = jnp.clip(jax.random.normal(jax.random.fold_in(key, 301), (NSPEC,), jnp.float32), -4.0, 4.0)
    magnitude = jax.random.uniform(jax.random.fold_in(key, 302), (NSPEC,), jnp.float32, 2.5, 3.5)
    return jnp.stack([energy, magnitude * signs], axis=1).astype(jnp.float32)


def block_scale(stream_key, extent, shards, low, largest):
    loudness = 1.0
    for position, shards_of in shards:
        steps = jax.random.uniform(jax.random.fold_in(jax.random.fold_in(stream_key, 6), position), (shards_of,), jnp.float32, low / len(shards), largest / len(shards))
        loudness = loudness * jnp.repeat(jnp.exp(steps), extent[position] // shards_of).reshape((-1,) + (1,) * (len(extent) - 1 - position))
    return loudness


def scatter_about(key, extent, width, most, shards=(), kind=jnp.bfloat16):
    level = block_scale(key, extent, shards, -0.22, 0.18) if shards else 1.0
    drawn = jax.random.normal(key, extent, jnp.float32) * width * level
    return jnp.minimum(jnp.maximum(drawn, -most), most).astype(kind)


def setup_inputs(seed: int = 0) -> dict:
    keys = jax.random.split(jax.random.key(seed), 12)
    return {
        "features": scatter_about(keys[0], (N_GX, N_GY, N_GZ, ATOMS, FEAT), 1.0, 6.0, ((0, 8), (1, 2), (2, 2))),
        "fraction": jnp.clip(0.98828125 * jax.random.uniform(keys[1], (N_GX, N_GY, N_GZ, 3, ATOMS), jnp.float32) ** block_scale(keys[1], (N_GX, N_GY, N_GZ, 3, ATOMS), ((0, 8), (1, 2), (2, 2)), -0.2, 0.2), 0.0, 0.98828125).astype(jnp.bfloat16),
        "cell_index": draw_cell_index(jax.random.fold_in(keys[11], 71), 0),
        "species": draw_species(jax.random.fold_in(keys[11], 71), 0),
        "octant_rows": draw_octant_rows(jax.random.fold_in(keys[11], 71), 0),
        "neighbours": draw_neighbours(jax.random.fold_in(keys[11], 71), 0),
        "radial_in": scatter_about(keys[6], (LAYERS, NB, HID), NB ** -0.5, 2.0),
        "radial_out": scatter_about(keys[7], (LAYERS, HID, FEAT), (HID // 4) ** -0.5, 1.5),
        "mix_weight": scatter_about(keys[8], (LAYERS, 2, C, C), C ** -0.5, 0.5),
        "readout": scatter_about(keys[9], (C, 2), (16 * C) ** -0.5, 0.125),
        "species_table": draw_species_table(jax.random.fold_in(keys[11], 71), 0),
    }


COULOMB = 4.0
EWALD = 0.7

def outer_cells():
    found = []
    for first in range(4):
        for second in range(4):
            for third in range(4):
                if 0 < first < 3 and 0 < second < 3 and (0 < third < 3):
                    continue
                found.append((first, second, third))
    return found

def offset_of(coord):
    return -1 if coord == 0 else 1 if coord == 3 else 0

def source_of(coord):
    return 1 if coord == 0 else 0 if coord == 3 else coord - 1

def spline(fraction_in):
    upper_t = fraction_in
    lower_t = 1.0 - fraction_in
    weights = jnp.stack([lower_t * lower_t * lower_t / 6.0, (3.0 * upper_t * upper_t * upper_t - 6.0 * upper_t * upper_t + 4.0) / 6.0, (-3.0 * upper_t * upper_t * upper_t + 3.0 * upper_t * upper_t + 3.0 * upper_t + 1.0) / 6.0, upper_t * upper_t * upper_t / 6.0])
    slopes = jnp.stack([-0.5 * lower_t * lower_t, 0.5 * (3.0 * upper_t * upper_t - 4.0 * upper_t), 0.5 * (-3.0 * upper_t * upper_t + 2.0 * upper_t + 1.0), 0.5 * upper_t * upper_t])
    return (weights, slopes)

def frequency(waves):
    signed = jnp.where(waves <= MESH // 2, waves, waves - MESH).astype(jnp.float32) / MESH
    modulus = 9.0 / jnp.square(2.0 + jnp.cos(waves.astype(jnp.float32) * (2.0 * math.pi / MESH)))
    return (signed, modulus)

def influence(wave_y, wave_z, wave_x):
    freq_y, modul_y = frequency(wave_y)
    freq_z, modul_z = frequency(wave_z)
    freq_x, modul_x = frequency(wave_x)
    wave_square = jnp.square(freq_x)[None, None, :] + jnp.square(freq_y)[:, None, None] + jnp.square(freq_z)[None, :, None]
    positive = wave_square > 0.0
    gaussian = jnp.exp(-(math.pi * math.pi / (EWALD * EWALD)) * wave_square)
    kernel = jnp.where(positive, gaussian / jnp.where(positive, wave_square, 1.0), 0.0)
    moduli = modul_x[None, None, :] * modul_y[:, None, None] * modul_z[None, :, None]
    return kernel * moduli * (COULOMB / (math.pi * MESH ** 3))

def interact(current, lookup, places, located, links, radial_in, radial_out, mix_weight):
    atom_count = current.shape[0]
    gathered = lookup[links].astype(jnp.float32)
    displace = places[links] - located[None]
    length_sq = lax.optimization_barrier(jnp.sum(displace * displace, axis=-1))
    distance = jnp.sqrt(length_sq)
    direction = displace / jnp.sqrt(length_sq + 1.0)[..., None]
    spacing = ENV / (NB - 1)
    centres = jnp.arange(NB, dtype=jnp.float32) * spacing
    envelope = jnp.square(jnp.maximum(1.0 - length_sq / (ENV * ENV), 0.0))
    basis_set = jnp.exp(-jnp.square((distance[..., None] - centres) / spacing)) * envelope[..., None]
    edge_count = NEIGH * atom_count
    hidden = jax.nn.silu(jnp.dot(basis_set.reshape(edge_count, NB).astype(jnp.bfloat16), radial_in, preferred_element_type=jnp.float32)).astype(jnp.bfloat16)
    radial = jnp.dot(hidden, radial_out, preferred_element_type=jnp.float32).reshape(NEIGH, atom_count, 4 * C)
    scalars = gathered[..., :C]
    vectors = gathered[..., C:].reshape(NEIGH, atom_count, 3, C)
    first_path = radial[..., :C]
    second_path = radial[..., C:2 * C]
    third_path = radial[..., 2 * C:3 * C]
    fourth_path = radial[..., 3 * C:]
    projected = lax.optimization_barrier(jnp.sum(direction[..., None] * vectors, axis=2))
    inverse_root = 1.0 / math.sqrt(NEIGH)
    scalar_message = lax.optimization_barrier(jnp.sum(first_path * scalars + second_path * projected, axis=0)) * inverse_root
    scaled_path = third_path * scalars
    vector_message = (jnp.einsum('kad,kac->adc', direction, scaled_path, precision=lax.Precision.HIGHEST) + lax.optimization_barrier(jnp.sum(fourth_path[:, :, None, :] * vectors, axis=0))) * inverse_root
    previous = current.astype(jnp.float32)
    scalar_new = previous[:, :C] + jax.nn.silu(jnp.dot(scalar_message.astype(jnp.bfloat16), mix_weight[0], preferred_element_type=jnp.float32))
    vector_new = previous[:, C:] + jnp.dot(vector_message.reshape(atom_count * 3, C).astype(jnp.bfloat16), mix_weight[1], preferred_element_type=jnp.float32).reshape(atom_count, 3 * C)
    return jnp.concatenate([scalar_new, vector_new], axis=1).astype(jnp.bfloat16)

def ghost_values(values, octant_rows):
    width_last = values.shape[-1]
    flattened = octant_rows.reshape(N_GX, N_GY, N_GZ, 8 * GHOST, 1)
    flattened = jnp.broadcast_to(flattened, (N_GX, N_GY, N_GZ, 8 * GHOST, width_last))
    buffers = jnp.take_along_axis(values, flattened, axis=3).reshape(N_GX, N_GY, N_GZ, 8, GHOST, width_last)
    pieces = []
    for corner in outer_cells():
        roll_by = (-offset_of(corner[0]), -offset_of(corner[1]), -offset_of(corner[2]))
        octant = 4 * source_of(corner[0]) + 2 * source_of(corner[1]) + source_of(corner[2])
        pieces.append(jnp.roll(buffers[:, :, :, octant], roll_by, (0, 1, 2)))
    return jnp.concatenate(pieces, axis=3)

def reference(features, fraction, cell_index, species, octant_rows, neighbours, radial_in, radial_out, mix_weight, readout, species_table):
    device_total = N_GX * N_GY * N_GZ
    cell_float = jnp.swapaxes(cell_index, 3, 4).astype(jnp.float32)
    fraction_float = jnp.swapaxes(fraction, 3, 4).astype(jnp.float32)
    located = cell_float + fraction_float
    shift_list = []
    for corner in outer_cells():
        shift_list.append(jnp.array([offset_of(corner[0]) * BX, offset_of(corner[1]) * BY, offset_of(corner[2]) * BZ], jnp.float32))
    shift_rows = jnp.repeat(jnp.stack(shift_list), GHOST, axis=0)
    ghost_places = ghost_values(cell_float, octant_rows) + shift_rows + ghost_values(fraction_float, octant_rows)
    places = jnp.concatenate([located, ghost_places, jnp.zeros((N_GX, N_GY, N_GZ, 1, 3), jnp.float32)], axis=3)
    corners = outer_cells()
    offset_x = jnp.array([offset_of(corner[0]) for corner in corners], jnp.int32)
    offset_y = jnp.array([offset_of(corner[1]) for corner in corners], jnp.int32)
    offset_z = jnp.array([offset_of(corner[2]) for corner in corners], jnp.int32)
    octant_ids = jnp.array([4 * source_of(corner[0]) + 2 * source_of(corner[1]) + source_of(corner[2]) for corner in corners], jnp.int32)
    current_features = features
    for layer_index in range(LAYERS):

        def per_device(inputs, layer_index=layer_index, whole=current_features):
            device_id, current, places_one, located_one, links_one = inputs
            index_x = device_id // (N_GY * N_GZ)
            index_y = device_id // N_GZ % N_GY
            index_z = device_id % N_GZ
            source_x = (index_x + offset_x) % N_GX
            source_y = (index_y + offset_y) % N_GY
            source_z = (index_z + offset_z) % N_GZ
            rows = octant_rows[source_x, source_y, source_z, octant_ids]
            arrived = whole[source_x[:, None], source_y[:, None], source_z[:, None], rows].reshape(56 * GHOST, 4 * C)
            lookup_one = jnp.concatenate([current, arrived, jnp.zeros((1, 4 * C), jnp.bfloat16)], axis=0)
            return interact(current, lookup_one, places_one, located_one, links_one, radial_in[layer_index], radial_out[layer_index], mix_weight[layer_index])
        mapped = lax.map(per_device, (jnp.arange(device_total, dtype=jnp.int32), current_features.reshape(device_total, ATOMS, 4 * C), places.reshape(device_total, NCAND + 1, 3), located.reshape(device_total, ATOMS, 3), neighbours.reshape(device_total, NEIGH, ATOMS)))
        current_features = mapped.reshape(N_GX, N_GY, N_GZ, ATOMS, 4 * C)
    scalars = current_features[..., :C].reshape(-1, C)
    head_out = jnp.dot(scalars, readout, preferred_element_type=jnp.float32).reshape(N_GX, N_GY, N_GZ, ATOMS, 2)
    one_hot = (species[..., None] == jnp.arange(NSPEC, dtype=jnp.int32)).astype(jnp.float32).reshape(-1, NSPEC)
    species_term = jnp.dot(one_hot, species_table, precision=lax.Precision.HIGHEST, preferred_element_type=jnp.float32).reshape(N_GX, N_GY, N_GZ, ATOMS, 2)
    base_energy = head_out[..., 0] + species_term[..., 0]
    charge = head_out[..., 1] + species_term[..., 1]
    weights, slopes = spline(fraction.astype(jnp.float32))
    anchors = [(jnp.arange(N_GX, dtype=jnp.int32) * BX).reshape(N_GX, 1, 1, 1), (jnp.arange(N_GY, dtype=jnp.int32) * BY).reshape(1, N_GY, 1, 1), (jnp.arange(N_GZ, dtype=jnp.int32) * BZ).reshape(1, 1, N_GZ, 1)]
    offsets = jnp.arange(4, dtype=jnp.int32).reshape(4, 1, 1, 1, 1)
    points = [(anchors[dim][None] + cell_index[:, :, :, dim][None] + offsets - 1) % MESH for dim in range(3)]
    weight_x = weights[:, :, :, :, 0]
    weight_y = weights[:, :, :, :, 1]
    weight_z = weights[:, :, :, :, 2]
    slope_x = slopes[:, :, :, :, 0]
    slope_y = slopes[:, :, :, :, 1]
    slope_z = slopes[:, :, :, :, 2]
    point_x = points[0][:, None, None]
    point_y = points[1][None, :, None]
    point_z = points[2][None, None, :]
    amount = charge[None, None, None] * weight_x[:, None, None] * weight_y[None, :, None] * weight_z[None, None, :]
    charge_mesh = jnp.zeros((MESH, MESH, MESH), jnp.float32).at[point_x, point_y, point_z].add(amount)
    waves = jnp.arange(MESH, dtype=jnp.int32)
    kernel = jnp.transpose(influence(waves, waves, waves), (2, 0, 1))
    spectrum = jnp.fft.fftn(charge_mesh)
    potential = jnp.real(jnp.fft.ifftn(spectrum * kernel)) * float(MESH ** 3)
    sampled = potential[point_x, point_y, point_z]
    potential_at = lax.optimization_barrier(jnp.sum(sampled * weight_x[:, None, None] * weight_y[None, :, None] * weight_z[None, None, :], axis=(0, 1, 2)))
    field_x = -lax.optimization_barrier(jnp.sum(sampled * slope_x[:, None, None] * weight_y[None, :, None] * weight_z[None, None, :], axis=(0, 1, 2)))
    field_y = -lax.optimization_barrier(jnp.sum(sampled * weight_x[:, None, None] * slope_y[None, :, None] * weight_z[None, None, :], axis=(0, 1, 2)))
    field_z = -lax.optimization_barrier(jnp.sum(sampled * weight_x[:, None, None] * weight_y[None, :, None] * slope_z[None, None, :], axis=(0, 1, 2)))
    recip_force = charge[:, :, :, None] * jnp.stack([field_x, field_y, field_z], axis=3)
    site_energy = base_energy + 0.5 * charge * potential_at
    return (current_features, site_energy, recip_force)
```

```python
import math

import jax
import jax.numpy as jnp
import numpy as np
from jax import lax
from jax.experimental import pallas as pl
from jax.experimental.pallas import tpu as pltpu
from jax.sharding import PartitionSpec as P

C = 128
NB = 8
LAYERS = 2
NEIGH = 16
ENV = 7
MESH = 256


COULOMB = 4.0
EWALD = 0.7
HIGHEST_PRECISION = lax.Precision.HIGHEST


def outer_cells():
    found = []
    for first in range(4):
        for second in range(4):
            for third in range(4):
                if 0 < first < 3 and 0 < second < 3 and (0 < third < 3):
                    continue
                found.append((first, second, third))
    return found


def offset_of(coord):
    return -1 if coord == 0 else 1 if coord == 3 else 0


def spline(fraction_in):
    lower_t = 1.0 - fraction_in
    weights = jnp.stack(
        [
            lower_t * lower_t * lower_t / 6.0,
            (3.0 * fraction_in * fraction_in * fraction_in - 6.0 * fraction_in * fraction_in + 4.0)
            / 6.0,
            (
                -3.0 * fraction_in * fraction_in * fraction_in
                + 3.0 * fraction_in * fraction_in
                + 3.0 * fraction_in
                + 1.0
            )
            / 6.0,
            fraction_in * fraction_in * fraction_in / 6.0,
        ]
    )
    slopes = jnp.stack(
        [
            -0.5 * lower_t * lower_t,
            0.5 * (3.0 * fraction_in * fraction_in - 4.0 * fraction_in),
            0.5 * (-3.0 * fraction_in * fraction_in + 2.0 * fraction_in + 1.0),
            0.5 * fraction_in * fraction_in,
        ]
    )
    return (weights, slopes)


def frequency(waves):
    signed = jnp.where(waves <= MESH // 2, waves, waves - MESH).astype(jnp.float32) / MESH
    modulus = 9.0 / jnp.square(2.0 + jnp.cos(waves.astype(jnp.float32) * (2.0 * math.pi / MESH)))
    return (signed, modulus)


def influence(wave_y, wave_z, wave_x):
    freq_y, modul_y = frequency(wave_y)
    freq_z, modul_z = frequency(wave_z)
    freq_x, modul_x = frequency(wave_x)
    wave_square = (
        jnp.square(freq_x)[None, None, :]
        + jnp.square(freq_y)[:, None, None]
        + jnp.square(freq_z)[None, :, None]
    )
    positive = wave_square > 0.0
    gaussian = jnp.exp(-(math.pi * math.pi / (EWALD * EWALD)) * wave_square)
    kernel = jnp.where(positive, gaussian / jnp.where(positive, wave_square, 1.0), 0.0)
    moduli = modul_x[None, None, :] * modul_y[:, None, None] * modul_z[None, :, None]
    return kernel * moduli * (COULOMB / (math.pi * MESH**3))


def phases(left, right):
    turns = left[:, None] * right[None, :] % MESH
    angle = turns.astype(jnp.float32) * (2.0 * math.pi / MESH)
    return (jnp.cos(angle), jnp.sin(angle))


AXES = ("gx", "gy", "gz")


def source_of(coord):
    return 1 if coord == 0 else 0 if coord == 3 else coord - 1


def layer_kernel(
    ids, links, feats, geo, own, own_geo, radial_in, radial_out, mix_weight, out, s_acc, v_acc
):
    step = pl.program_id(0)
    atom_count = own.shape[0]

    @pl.when(step == 0)
    def _():
        s_acc[...] = jnp.zeros_like(s_acc)
        v_acc[...] = jnp.zeros_like(v_acc)

    picked = (links[...] == ids[...]).astype(jnp.float32).astype(jnp.bfloat16)
    rows = jnp.dot(picked, feats[...], preferred_element_type=jnp.float32)
    spots = jnp.dot(picked, geo[...], preferred_element_type=jnp.float32)
    edges = rows.shape[0]
    slots = edges // atom_count
    here = own_geo[...].astype(jnp.float32)
    located = jnp.concatenate([here[:, 0:3] + here[:, 3:6]] * slots, axis=0)
    displace = spots[:, 0:3] + spots[:, 3:6] - located
    length_sq = jnp.sum(displace * displace, axis=1, keepdims=True)
    distance = jnp.sqrt(length_sq)
    direction = displace / jnp.sqrt(length_sq + 1.0)
    spacing = ENV / (NB - 1)
    centres = lax.broadcasted_iota(jnp.int32, (edges, C), 1).astype(jnp.float32) * spacing
    envelope = jnp.square(jnp.maximum(1.0 - length_sq / (ENV * ENV), 0.0))
    basis = jnp.exp(-jnp.square((distance - centres) / spacing)) * envelope
    hidden = jnp.dot(
        basis.astype(jnp.bfloat16), radial_in[...], preferred_element_type=jnp.float32
    )
    hidden = (hidden / (1.0 + jnp.exp(-hidden))).astype(jnp.bfloat16)
    radial = jnp.dot(hidden, radial_out[...], preferred_element_type=jnp.float32)
    scalars = rows[:, :C]
    units = [direction[:, d : d + 1] for d in range(3)]
    vectors = [rows[:, C * (d + 1) : C * (d + 2)] for d in range(3)]
    projected = units[0] * vectors[0] + units[1] * vectors[1] + units[2] * vectors[2]
    scaled = radial[:, 2 * C : 3 * C] * scalars
    fourth = radial[:, 3 * C :]

    def over_slots(edge_values):
        return sum(edge_values[k * atom_count : (k + 1) * atom_count] for k in range(slots))

    s_acc[...] += over_slots(radial[:, :C] * scalars + radial[:, C : 2 * C] * projected)
    for d in range(3):
        v_acc[d] += over_slots(units[d] * scaled + fourth * vectors[d])

    @pl.when(step == pl.num_programs(0) - 1)
    def _():
        inverse_root = 1.0 / math.sqrt(NEIGH)
        previous = own[...].astype(jnp.float32)
        message = (s_acc[...] * inverse_root).astype(jnp.bfloat16)
        mixed = jnp.dot(message, mix_weight[0], preferred_element_type=jnp.float32)
        out[:, :C] = (previous[:, :C] + mixed / (1.0 + jnp.exp(-mixed))).astype(jnp.bfloat16)
        for d in range(3):
            message = (v_acc[d] * inverse_root).astype(jnp.bfloat16)
            mixed = jnp.dot(message, mix_weight[1], preferred_element_type=jnp.float32)
            span = slice(C * (d + 1), C * (d + 2))
            out[:, span] = (previous[:, span] + mixed).astype(jnp.bfloat16)


def layer(ids, links, feats, geo, own, own_geo, radial_in, radial_out, mix_weight):
    atom_count = own.shape[0]
    edge_block = 4 * atom_count
    whole = lambda array: pl.BlockSpec(array.shape, lambda i: (0,) * array.ndim)
    return pl.pallas_call(
        layer_kernel,
        grid=(links.shape[0] // edge_block,),
        out_shape=jax.ShapeDtypeStruct(own.shape, jnp.bfloat16),
        in_specs=[
            whole(ids),
            pl.BlockSpec((edge_block, 1), lambda i: (i, 0)),
            whole(feats),
            whole(geo),
            whole(own),
            whole(own_geo),
            whole(radial_in),
            whole(radial_out),
            whole(mix_weight),
        ],
        out_specs=pl.BlockSpec(own.shape, lambda i: (0, 0)),
        scratch_shapes=[
            pltpu.VMEM((atom_count, C), jnp.float32),
            pltpu.VMEM((3, atom_count, C), jnp.float32),
        ],
        compiler_params=pltpu.CompilerParams(
            dimension_semantics=("arbitrary",), vmem_limit_bytes=40 * 1024 * 1024
        ),
    )(ids, links, feats, geo, own, own_geo, radial_in, radial_out, mix_weight)


def ghost_plan(counts):
    groups = {}
    for number, corner in enumerate(outer_cells()):
        offset = tuple(offset_of(coord) for coord in corner)
        bits = [source_of(coord) for coord in corner]
        octant = 4 * bits[0] + 2 * bits[1] + bits[2]
        key = tuple(o % n for o, n in zip(offset, counts))
        groups.setdefault(key, []).append((number, octant, offset))
    return groups


def exchange(buffers, counts, groups):
    pieces = []
    devices = list(np.ndindex(*counts))
    linear = lambda spot: (spot[0] * counts[1] + spot[1]) * counts[2] + spot[2]
    for key, members in groups.items():
        octants = [member[1] for member in members]
        if octants == list(range(8)):
            block = buffers
        else:
            block = jnp.concatenate([buffers[o : o + 1] for o in octants], axis=0)
        if any(key):
            route = []
            for spot in devices:
                source = tuple((a + o) % n for a, o, n in zip(spot, key, counts))
                route.append((linear(source), linear(spot)))
            block = lax.ppermute(block, AXES, route)
        pieces.append(block)
    return jnp.concatenate(pieces, axis=0)


def cas_table(left, right):
    cosine, sine = phases(left, right)
    return cosine + sine


def local_rows(coefficient, first, span):
    slot_index = jnp.arange(span, dtype=jnp.int32)[None, :, None]
    summed = 0.0
    for offset in range(4):
        summed = summed + jnp.where(
            slot_index == ((first + offset) % MESH)[:, None, :], coefficient[offset][:, None, :], 0.0
        )
    return summed


def mm(pattern, left, right):
    return jnp.einsum(
        pattern, left, right, precision=lax.Precision.HIGH, preferred_element_type=jnp.float32
    )


def per_device(
    features,
    fraction,
    cell_index,
    species,
    octant_rows,
    neighbours,
    radial_in,
    radial_out,
    mix_weight,
    readout,
    species_table,
):
    bf16 = jnp.bfloat16
    current = features[0, 0, 0]
    fraction_here = fraction[0, 0, 0]
    cells_here = cell_index[0, 0, 0]
    kinds = species[0, 0, 0]
    chosen_rows = octant_rows[0, 0, 0].reshape(-1)
    links = neighbours[0, 0, 0].reshape(-1, 1)
    atom_count, feat_width = current.shape
    ghost_count = chosen_rows.shape[0] // 8
    counts = tuple(lax.axis_size(axis) for axis in AXES)
    count_x, count_y, count_z = counts
    total = count_x * count_y * count_z
    span_x, span_y, span_z = (MESH // n for n in counts)
    small = jnp.concatenate([cells_here.astype(bf16), fraction_here], axis=0)
    everyone = lax.all_gather(small, AXES, axis=0, tiled=False)
    own_geo = jnp.pad(jnp.transpose(small), ((0, 0), (0, C - 6)))
    pick = (chosen_rows[:, None] == jnp.arange(atom_count, dtype=jnp.int32)[None, :]).astype(bf16)
    groups = ghost_plan(counts)
    ids = list(range(atom_count))
    shift_rows = []
    for members in groups.values():
        for number, _, offset in members:
            ids += [atom_count + number * ghost_count + r for r in range(ghost_count)]
            shift = [o * w for o, w in zip(offset, (span_x, span_y, span_z))]
            shift_rows += [shift] * ghost_count
    real_rows = len(ids)
    table_rows = -(-real_rows // 128) * 128
    ids = jnp.asarray(np.array(ids + [-1] * (table_rows - real_rows), np.int32))[None, :]
    shift_rows = np.pad(np.array(shift_rows, np.float32), ((0, 0), (0, C - 3)))
    fill = table_rows - real_rows

    def outgoing(values):
        return jnp.dot(pick, values, preferred_element_type=jnp.float32).astype(bf16).reshape(
            8, ghost_count, -1
        )

    geo = own_geo
    for index in range(LAYERS):
        values = jnp.concatenate([current, own_geo], axis=1) if index == 0 else current
        arrived = exchange(outgoing(values), counts, groups).reshape(
            real_rows - atom_count, values.shape[1]
        )
        feats = jnp.concatenate(
            [current, arrived[:, :feat_width], jnp.zeros((fill, feat_width), bf16)], axis=0
        )
        if index == 0:
            ghost_geo = (arrived[:, feat_width:].astype(jnp.float32) + shift_rows).astype(bf16)
            geo = jnp.concatenate([own_geo, ghost_geo, jnp.zeros((fill, C), bf16)], axis=0)
        first_pad = jnp.pad(radial_in[index], ((0, C - NB), (0, C - radial_in.shape[2])))
        second_pad = jnp.pad(radial_out[index], ((0, C - radial_out.shape[1]), (0, 0)))
        current = layer(
            ids, links, feats, geo, current, own_geo, first_pad, second_pad, mix_weight[index]
        )

    head_out = jnp.dot(current[:, :C], readout, preferred_element_type=jnp.float32)
    one_hot = (
        kinds[:, None] == jnp.arange(species_table.shape[0], dtype=jnp.int32)[None, :]
    ).astype(jnp.float32)
    species_term = jnp.dot(
        one_hot, species_table, precision=HIGHEST_PRECISION, preferred_element_type=jnp.float32
    )
    base_energy = head_out[:, 0] + species_term[:, 0]
    charge = head_out[:, 1] + species_term[:, 1]
    charges = lax.all_gather(charge, AXES, axis=0, tiled=False).reshape(count_x, -1)

    device = (lax.axis_index("gx") * count_y + lax.axis_index("gy")) * count_z
    device = device + lax.axis_index("gz")
    wave_count = MESH // total
    waves_y = device * wave_count + jnp.arange(wave_count, dtype=jnp.int32)
    full = jnp.arange(MESH, dtype=jnp.int32)
    table = everyone.reshape(count_x, count_y * count_z, 6, atom_count)
    table = jnp.transpose(table, (2, 0, 1, 3)).reshape(6, count_x, -1).astype(jnp.float32)
    all_cells = table[:3].astype(jnp.int32)
    weights, slopes = spline(table[3:])
    order = jnp.arange(count_y * count_z * atom_count, dtype=jnp.int32) // atom_count
    start_y = (order // count_z * span_y)[None, :]
    start_z = (order % count_z * span_z)[None, :]
    width_x = -(-(span_x + 3) // 8) * 8
    weight_x = local_rows(weights[:, 0], all_cells[0], width_x)
    slope_x = local_rows(slopes[:, 0], all_cells[0], width_x)
    first_z = all_cells[2] + start_z + (MESH - 1)
    weight_z = local_rows(weights[:, 2], first_z, MESH)
    slope_z = local_rows(slopes[:, 2], first_z, MESH)
    place_y = all_cells[1] + start_y
    turns = (waves_y[:, None, None] * place_y[None]) % MESH
    angle = turns.astype(jnp.float32) * (2.0 * math.pi / MESH)
    cosine_y, sine_y = jnp.cos(angle), jnp.sin(angle)
    step_cosine, step_sine = phases(waves_y, jnp.arange(4, dtype=jnp.int32) - 1 + MESH)
    plus, minus = step_cosine + step_sine, step_cosine - step_sine

    def along_y(values):
        first = sum(plus[:, m][:, None, None] * values[m][None] for m in range(4))
        second = sum(minus[:, m][:, None, None] * values[m][None] for m in range(4))
        return cosine_y * first + sine_y * second

    weight_y = along_y(weights[:, 1])
    slope_y = along_y(slopes[:, 1])
    slots_x = (
        jnp.arange(count_x, dtype=jnp.int32)[:, None] * span_x
        + jnp.arange(width_x, dtype=jnp.int32)[None, :]
        + (MESH - 1)
    ).reshape(-1) % MESH
    cas_x = cas_table(full, slots_x).reshape(MESH, count_x, width_x)
    cas_z = cas_table(full, full)
    influence_here = influence(waves_y, full, full)

    loaded = (jnp.transpose(weight_y, (1, 0, 2)) * charges[:, None, :])[:, :, None, :]
    loaded = loaded * weight_x[:, None, :, :]
    spread = mm("ikxa,iza->ikxz", loaded, weight_z)
    spectrum = mm("ikxz,zw->ikxw", spread, cas_z)
    spectrum = mm("vix,ikxw->kwv", cas_x, spectrum) * influence_here
    back = mm("vix,kwv->ikxw", cas_x, spectrum)
    back = mm("ikxw,wz->ikxz", back, cas_z)
    level = mm("ikxz,iza->ikxa", back, weight_z)
    level_slope = mm("ikxz,iza->ikxa", back, slope_z)
    by_x = jnp.transpose(jnp.sum(level * weight_x[:, None], axis=2), (1, 0, 2))
    by_slope_x = jnp.transpose(jnp.sum(level * slope_x[:, None], axis=2), (1, 0, 2))
    by_slope_z = jnp.transpose(jnp.sum(level_slope * weight_x[:, None], axis=2), (1, 0, 2))
    partial = jnp.stack(
        [
            jnp.sum(weight_y * by_x, axis=0),
            jnp.sum(weight_y * by_slope_x, axis=0),
            jnp.sum(slope_y * by_x, axis=0),
            jnp.sum(weight_y * by_slope_z, axis=0),
        ]
    )
    partial = jnp.transpose(partial.reshape(4, total, atom_count), (1, 0, 2))
    mine = lax.psum_scatter(partial, AXES, scatter_dimension=0, tiled=False)
    recip_force = -charge[None, :] * mine[1:]
    site_energy = base_energy + 0.5 * charge * mine[0]
    return (current[None, None, None], site_energy[None, None, None], recip_force[None, None, None])


def solution(mesh):
    in_specs = (
        P("gx", "gy", "gz", None, None),
        P("gx", "gy", "gz", None, None),
        P("gx", "gy", "gz", None, None),
        P("gx", "gy", "gz", None),
        P("gx", "gy", "gz", None, None),
        P("gx", "gy", "gz", None, None),
        P(),
        P(),
        P(),
        P(),
        P(),
    )
    out_specs = (
        P("gx", "gy", "gz", None, None),
        P("gx", "gy", "gz", None),
        P("gx", "gy", "gz", None, None),
    )
    return jax.shard_map(
        per_device, mesh=mesh, in_specs=in_specs, out_specs=out_specs, check_vma=False
    )
```

```python
import math

import jax
import jax.numpy as jnp
import numpy as np
from jax import lax
from jax.experimental import pallas as pl
from jax.experimental.pallas import tpu as pltpu
from jax.sharding import PartitionSpec as P

C = 128
NB = 8
LAYERS = 2
NEIGH = 16
ENV = 7
MESH = 256


COULOMB = 4.0
EWALD = 0.7
HIGHEST_PRECISION = lax.Precision.HIGHEST


def outer_cells():
    found = []
    for first in range(4):
        for second in range(4):
            for third in range(4):
                if 0 < first < 3 and 0 < second < 3 and (0 < third < 3):
                    continue
                found.append((first, second, third))
    return found


def offset_of(coord):
    return -1 if coord == 0 else 1 if coord == 3 else 0


def spline(fraction_in):
    lower_t = 1.0 - fraction_in
    weights = jnp.stack(
        [
            lower_t * lower_t * lower_t / 6.0,
            (3.0 * fraction_in * fraction_in * fraction_in - 6.0 * fraction_in * fraction_in + 4.0)
            / 6.0,
            (
                -3.0 * fraction_in * fraction_in * fraction_in
                + 3.0 * fraction_in * fraction_in
                + 3.0 * fraction_in
                + 1.0
            )
            / 6.0,
            fraction_in * fraction_in * fraction_in / 6.0,
        ]
    )
    slopes = jnp.stack(
        [
            -0.5 * lower_t * lower_t,
            0.5 * (3.0 * fraction_in * fraction_in - 4.0 * fraction_in),
            0.5 * (-3.0 * fraction_in * fraction_in + 2.0 * fraction_in + 1.0),
            0.5 * fraction_in * fraction_in,
        ]
    )
    return (weights, slopes)


def frequency(waves):
    signed = jnp.where(waves <= MESH // 2, waves, waves - MESH).astype(jnp.float32) / MESH
    modulus = 9.0 / jnp.square(2.0 + jnp.cos(waves.astype(jnp.float32) * (2.0 * math.pi / MESH)))
    return (signed, modulus)


def influence(wave_y, wave_z, wave_x):
    freq_y, modul_y = frequency(wave_y)
    freq_z, modul_z = frequency(wave_z)
    freq_x, modul_x = frequency(wave_x)
    wave_square = (
        jnp.square(freq_x)[None, None, :]
        + jnp.square(freq_y)[:, None, None]
        + jnp.square(freq_z)[None, :, None]
    )
    positive = wave_square > 0.0
    gaussian = jnp.exp(-(math.pi * math.pi / (EWALD * EWALD)) * wave_square)
    kernel = jnp.where(positive, gaussian / jnp.where(positive, wave_square, 1.0), 0.0)
    moduli = modul_x[None, None, :] * modul_y[:, None, None] * modul_z[None, :, None]
    return kernel * moduli * (COULOMB / (math.pi * MESH**3))


def phases(left, right):
    turns = left[:, None] * right[None, :] % MESH
    angle = turns.astype(jnp.float32) * (2.0 * math.pi / MESH)
    return (jnp.cos(angle), jnp.sin(angle))


AXES = ("gx", "gy", "gz")


def source_of(coord):
    return 1 if coord == 0 else 0 if coord == 3 else coord - 1


def layer_kernel(
    ids, links, feats, geo, own, own_geo, radial_in, radial_out, mix_weight, out, s_acc, v_acc
):
    step = pl.program_id(0)
    atom_count = own.shape[0]

    @pl.when(step == 0)
    def _():
        s_acc[...] = jnp.zeros_like(s_acc)
        v_acc[...] = jnp.zeros_like(v_acc)

    picked = (links[...] == ids[...]).astype(jnp.float32).astype(jnp.bfloat16)
    rows = jnp.dot(picked, feats[...], preferred_element_type=jnp.float32)
    spots = jnp.dot(picked, geo[...], preferred_element_type=jnp.float32)
    edges = rows.shape[0]
    slots = edges // atom_count
    here = own_geo[...].astype(jnp.float32)
    located = jnp.concatenate([here[:, 0:3] + here[:, 3:6]] * slots, axis=0)
    displace = spots[:, 0:3] + spots[:, 3:6] - located
    length_sq = jnp.sum(displace * displace, axis=1, keepdims=True)
    distance = jnp.sqrt(length_sq)
    direction = displace / jnp.sqrt(length_sq + 1.0)
    spacing = ENV / (NB - 1)
    centres = lax.broadcasted_iota(jnp.int32, (edges, C), 1).astype(jnp.float32) * spacing
    envelope = jnp.square(jnp.maximum(1.0 - length_sq / (ENV * ENV), 0.0))
    basis = jnp.exp(-jnp.square((distance - centres) / spacing)) * envelope
    hidden = jnp.dot(
        basis.astype(jnp.bfloat16), radial_in[...], preferred_element_type=jnp.float32
    )
    hidden = (hidden / (1.0 + jnp.exp(-hidden))).astype(jnp.bfloat16)
    radial = jnp.dot(hidden, radial_out[...], preferred_element_type=jnp.float32)
    scalars = rows[:, :C]
    units = [direction[:, d : d + 1] for d in range(3)]
    vectors = [rows[:, C * (d + 1) : C * (d + 2)] for d in range(3)]
    projected = units[0] * vectors[0] + units[1] * vectors[1] + units[2] * vectors[2]
    scaled = radial[:, 2 * C : 3 * C] * scalars
    fourth = radial[:, 3 * C :]

    def over_slots(edge_values):
        return sum(edge_values[k * atom_count : (k + 1) * atom_count] for k in range(slots))

    s_acc[...] += over_slots(radial[:, :C] * scalars + radial[:, C : 2 * C] * projected)
    for d in range(3):
        v_acc[d] += over_slots(units[d] * scaled + fourth * vectors[d])

    @pl.when(step == pl.num_programs(0) - 1)
    def _():
        inverse_root = 1.0 / math.sqrt(NEIGH)
        previous = own[...].astype(jnp.float32)
        message = (s_acc[...] * inverse_root).astype(jnp.bfloat16)
        mixed = jnp.dot(message, mix_weight[0], preferred_element_type=jnp.float32)
        out[:, :C] = (previous[:, :C] + mixed / (1.0 + jnp.exp(-mixed))).astype(jnp.bfloat16)
        for d in range(3):
            message = (v_acc[d] * inverse_root).astype(jnp.bfloat16)
            mixed = jnp.dot(message, mix_weight[1], preferred_element_type=jnp.float32)
            span = slice(C * (d + 1), C * (d + 2))
            out[:, span] = (previous[:, span] + mixed).astype(jnp.bfloat16)


def layer(ids, links, feats, geo, own, own_geo, radial_in, radial_out, mix_weight):
    atom_count = own.shape[0]
    edge_block = 4 * atom_count
    whole = lambda array: pl.BlockSpec(array.shape, lambda i: (0,) * array.ndim)
    return pl.pallas_call(
        layer_kernel,
        grid=(links.shape[0] // edge_block,),
        out_shape=jax.ShapeDtypeStruct(own.shape, jnp.bfloat16),
        in_specs=[
            whole(ids),
            pl.BlockSpec((edge_block, 1), lambda i: (i, 0)),
            whole(feats),
            whole(geo),
            whole(own),
            whole(own_geo),
            whole(radial_in),
            whole(radial_out),
            whole(mix_weight),
        ],
        out_specs=pl.BlockSpec(own.shape, lambda i: (0, 0)),
        scratch_shapes=[
            pltpu.VMEM((atom_count, C), jnp.float32),
            pltpu.VMEM((3, atom_count, C), jnp.float32),
        ],
        compiler_params=pltpu.CompilerParams(
            dimension_semantics=("arbitrary",), vmem_limit_bytes=40 * 1024 * 1024
        ),
    )(ids, links, feats, geo, own, own_geo, radial_in, radial_out, mix_weight)


def ghost_plan(counts):
    groups = {}
    for number, corner in enumerate(outer_cells()):
        offset = tuple(offset_of(coord) for coord in corner)
        bits = [source_of(coord) for coord in corner]
        octant = 4 * bits[0] + 2 * bits[1] + bits[2]
        key = tuple(o % n for o, n in zip(offset, counts))
        groups.setdefault(key, []).append((number, octant, offset))
    return groups


def exchange(buffers, counts, groups):
    pieces = []
    devices = list(np.ndindex(*counts))
    linear = lambda spot: (spot[0] * counts[1] + spot[1]) * counts[2] + spot[2]
    for key, members in groups.items():
        octants = [member[1] for member in members]
        if octants == list(range(8)):
            block = buffers
        else:
            block = jnp.concatenate([buffers[o : o + 1] for o in octants], axis=0)
        if any(key):
            route = []
            for spot in devices:
                source = tuple((a + o) % n for a, o, n in zip(spot, key, counts))
                route.append((linear(source), linear(spot)))
            block = lax.ppermute(block, AXES, route)
        pieces.append(block)
    return jnp.concatenate(pieces, axis=0)


def shifted(block, axes, count, step):
    return lax.ppermute(block, axes, [((i + step) % count, i) for i in range(count)])


def gather_from(block, axes):
    count, me = lax.axis_size(axes), lax.axis_index(axes)
    pieces = [block] + [shifted(block, axes, count, step) for step in range(1, count)]
    return lax.dynamic_slice_in_dim(jnp.stack(pieces + pieces), count - me, count, 0)


def sum_to(blocks, axes):
    count, me = lax.axis_size(axes), lax.axis_index(axes)
    turned = lax.dynamic_slice_in_dim(jnp.concatenate([blocks, blocks]), me, count, 0)
    return turned[0] + sum(
        shifted(turned[step], axes, count, count - step) for step in range(1, count)
    )


def cas_table(left, right):
    cosine, sine = phases(left, right)
    return cosine + sine


def local_rows(coefficient, first, span):
    slot_index = jnp.arange(span, dtype=jnp.int32)[None, :, None]
    summed = 0.0
    for offset in range(4):
        summed = summed + jnp.where(
            slot_index == ((first + offset) % MESH)[:, None, :], coefficient[offset][:, None, :], 0.0
        )
    return summed


def mm(pattern, left, right):
    return jnp.einsum(
        pattern, left, right, precision=lax.Precision.HIGH, preferred_element_type=jnp.float32
    )


def per_device(
    features,
    fraction,
    cell_index,
    species,
    octant_rows,
    neighbours,
    radial_in,
    radial_out,
    mix_weight,
    readout,
    species_table,
):
    bf16 = jnp.bfloat16
    current = features[0, 0, 0]
    fraction_here = fraction[0, 0, 0]
    cells_here = cell_index[0, 0, 0]
    kinds = species[0, 0, 0]
    chosen_rows = octant_rows[0, 0, 0].reshape(-1)
    links = neighbours[0, 0, 0].reshape(-1, 1)
    atom_count, feat_width = current.shape
    ghost_count = chosen_rows.shape[0] // 8
    counts = tuple(lax.axis_size(axis) for axis in AXES)
    count_x, count_y, count_z = counts
    total = count_x * count_y * count_z
    span_x, span_y, span_z = (MESH // n for n in counts)
    small = jnp.concatenate([cells_here.astype(bf16), fraction_here], axis=0)
    everyone = gather_from(gather_from(small, ("gy", "gz")), ("gx",))
    own_geo = jnp.pad(jnp.transpose(small), ((0, 0), (0, C - 6)))
    pick = (chosen_rows[:, None] == jnp.arange(atom_count, dtype=jnp.int32)[None, :]).astype(bf16)
    groups = ghost_plan(counts)
    ids = list(range(atom_count))
    shift_rows = []
    for members in groups.values():
        for number, _, offset in members:
            ids += [atom_count + number * ghost_count + r for r in range(ghost_count)]
            shift = [o * w for o, w in zip(offset, (span_x, span_y, span_z))]
            shift_rows += [shift] * ghost_count
    real_rows = len(ids)
    table_rows = -(-real_rows // 128) * 128
    ids = jnp.asarray(np.array(ids + [-1] * (table_rows - real_rows), np.int32))[None, :]
    shift_rows = np.pad(np.array(shift_rows, np.float32), ((0, 0), (0, C - 3)))
    fill = table_rows - real_rows

    def outgoing(values):
        return jnp.dot(pick, values, preferred_element_type=jnp.float32).astype(bf16).reshape(
            8, ghost_count, -1
        )

    geo = own_geo
    for index in range(LAYERS):
        values = jnp.concatenate([current, own_geo], axis=1) if index == 0 else current
        arrived = exchange(outgoing(values), counts, groups).reshape(
            real_rows - atom_count, values.shape[1]
        )
        feats = jnp.concatenate(
            [current, arrived[:, :feat_width], jnp.zeros((fill, feat_width), bf16)], axis=0
        )
        if index == 0:
            ghost_geo = (arrived[:, feat_width:].astype(jnp.float32) + shift_rows).astype(bf16)
            geo = jnp.concatenate([own_geo, ghost_geo, jnp.zeros((fill, C), bf16)], axis=0)
        first_pad = jnp.pad(radial_in[index], ((0, C - NB), (0, C - radial_in.shape[2])))
        second_pad = jnp.pad(radial_out[index], ((0, C - radial_out.shape[1]), (0, 0)))
        current = layer(
            ids, links, feats, geo, current, own_geo, first_pad, second_pad, mix_weight[index]
        )

    head_out = jnp.dot(current[:, :C], readout, preferred_element_type=jnp.float32)
    one_hot = (
        kinds[:, None] == jnp.arange(species_table.shape[0], dtype=jnp.int32)[None, :]
    ).astype(jnp.float32)
    species_term = jnp.dot(
        one_hot, species_table, precision=HIGHEST_PRECISION, preferred_element_type=jnp.float32
    )
    base_energy = head_out[:, 0] + species_term[:, 0]
    charge = head_out[:, 1] + species_term[:, 1]
    charges = gather_from(gather_from(charge[None], ("gy", "gz")), ("gx",)).reshape(count_x, -1)

    device = (lax.axis_index("gx") * count_y + lax.axis_index("gy")) * count_z
    device = device + lax.axis_index("gz")
    wave_count = MESH // total
    waves_y = device * wave_count + jnp.arange(wave_count, dtype=jnp.int32)
    full = jnp.arange(MESH, dtype=jnp.int32)
    table = everyone.reshape(count_x, count_y * count_z, 6, atom_count)
    table = jnp.transpose(table, (2, 0, 1, 3)).reshape(6, count_x, -1).astype(jnp.float32)
    all_cells = table[:3].astype(jnp.int32)
    weights, slopes = spline(table[3:])
    order = jnp.arange(count_y * count_z * atom_count, dtype=jnp.int32) // atom_count
    start_y = (order // count_z * span_y)[None, :]
    start_z = (order % count_z * span_z)[None, :]
    width_x = -(-(span_x + 3) // 8) * 8
    weight_x = local_rows(weights[:, 0], all_cells[0], width_x)
    slope_x = local_rows(slopes[:, 0], all_cells[0], width_x)
    first_z = all_cells[2] + start_z + (MESH - 1)
    weight_z = local_rows(weights[:, 2], first_z, MESH)
    slope_z = local_rows(slopes[:, 2], first_z, MESH)
    place_y = all_cells[1] + start_y
    turns = (waves_y[:, None, None] * place_y[None]) % MESH
    angle = turns.astype(jnp.float32) * (2.0 * math.pi / MESH)
    cosine_y, sine_y = jnp.cos(angle), jnp.sin(angle)
    step_cosine, step_sine = phases(waves_y, jnp.arange(4, dtype=jnp.int32) - 1 + MESH)
    plus, minus = step_cosine + step_sine, step_cosine - step_sine

    def along_y(values):
        first = sum(plus[:, m][:, None, None] * values[m][None] for m in range(4))
        second = sum(minus[:, m][:, None, None] * values[m][None] for m in range(4))
        return cosine_y * first + sine_y * second

    weight_y = along_y(weights[:, 1])
    slope_y = along_y(slopes[:, 1])
    slots_x = (
        jnp.arange(count_x, dtype=jnp.int32)[:, None] * span_x
        + jnp.arange(width_x, dtype=jnp.int32)[None, :]
        + (MESH - 1)
    ).reshape(-1) % MESH
    cas_x = cas_table(full, slots_x).reshape(MESH, count_x, width_x)
    cas_z = cas_table(full, full)
    influence_here = influence(waves_y, full, full)

    loaded = (jnp.transpose(weight_y, (1, 0, 2)) * charges[:, None, :])[:, :, None, :]
    loaded = loaded * weight_x[:, None, :, :]
    spread = mm("ikxa,iza->ikxz", loaded, weight_z)
    spectrum = mm("ikxz,zw->ikxw", spread, cas_z)
    spectrum = mm("vix,ikxw->kwv", cas_x, spectrum) * influence_here
    back = mm("vix,kwv->ikxw", cas_x, spectrum)
    back = mm("ikxw,wz->ikxz", back, cas_z)
    level = mm("ikxz,iza->ikxa", back, weight_z)
    level_slope = mm("ikxz,iza->ikxa", back, slope_z)
    by_x = jnp.transpose(jnp.sum(level * weight_x[:, None], axis=2), (1, 0, 2))
    by_slope_x = jnp.transpose(jnp.sum(level * slope_x[:, None], axis=2), (1, 0, 2))
    by_slope_z = jnp.transpose(jnp.sum(level_slope * weight_x[:, None], axis=2), (1, 0, 2))
    partial = jnp.stack(
        [
            jnp.sum(weight_y * by_x, axis=0),
            jnp.sum(weight_y * by_slope_x, axis=0),
            jnp.sum(slope_y * by_x, axis=0),
            jnp.sum(weight_y * by_slope_z, axis=0),
        ]
    )
    partial = jnp.transpose(
        partial.reshape(4, count_x, count_y * count_z, atom_count), (1, 2, 0, 3)
    )
    mine = sum_to(sum_to(partial, ("gx",)), ("gy", "gz"))
    recip_force = -charge[None, :] * mine[1:]
    site_energy = base_energy + 0.5 * charge * mine[0]
    return (current[None, None, None], site_energy[None, None, None], recip_force[None, None, None])


def solution(mesh):
    in_specs = (
        P("gx", "gy", "gz", None, None),
        P("gx", "gy", "gz", None, None),
        P("gx", "gy", "gz", None, None),
        P("gx", "gy", "gz", None),
        P("gx", "gy", "gz", None, None),
        P("gx", "gy", "gz", None, None),
        P(),
        P(),
        P(),
        P(),
        P(),
    )
    out_specs = (
        P("gx", "gy", "gz", None, None),
        P("gx", "gy", "gz", None),
        P("gx", "gy", "gz", None, None),
    )
    return jax.shard_map(
        per_device, mesh=mesh, in_specs=in_specs, out_specs=out_specs, check_vma=False
    )
```

```python
import math

import jax
import jax.numpy as jnp
import numpy as np
from jax import lax
from jax.experimental import pallas as pl
from jax.experimental.pallas import tpu as pltpu
from jax.sharding import PartitionSpec as P

C = 128
NB = 8
LAYERS = 2
NEIGH = 16
ENV = 7
MESH = 256


COULOMB = 4.0
EWALD = 0.7
HIGHEST_PRECISION = lax.Precision.HIGHEST


def outer_cells():
    found = []
    for first in range(4):
        for second in range(4):
            for third in range(4):
                if 0 < first < 3 and 0 < second < 3 and (0 < third < 3):
                    continue
                found.append((first, second, third))
    return found


def offset_of(coord):
    return -1 if coord == 0 else 1 if coord == 3 else 0


def spline(fraction_in):
    lower_t = 1.0 - fraction_in
    weights = jnp.stack(
        [
            lower_t * lower_t * lower_t / 6.0,
            (3.0 * fraction_in * fraction_in * fraction_in - 6.0 * fraction_in * fraction_in + 4.0)
            / 6.0,
            (
                -3.0 * fraction_in * fraction_in * fraction_in
                + 3.0 * fraction_in * fraction_in
                + 3.0 * fraction_in
                + 1.0
            )
            / 6.0,
            fraction_in * fraction_in * fraction_in / 6.0,
        ]
    )
    slopes = jnp.stack(
        [
            -0.5 * lower_t * lower_t,
            0.5 * (3.0 * fraction_in * fraction_in - 4.0 * fraction_in),
            0.5 * (-3.0 * fraction_in * fraction_in + 2.0 * fraction_in + 1.0),
            0.5 * fraction_in * fraction_in,
        ]
    )
    return (weights, slopes)


def frequency(waves):
    signed = jnp.where(waves <= MESH // 2, waves, waves - MESH).astype(jnp.float32) / MESH
    modulus = 9.0 / jnp.square(2.0 + jnp.cos(waves.astype(jnp.float32) * (2.0 * math.pi / MESH)))
    return (signed, modulus)


def influence(wave_y, wave_z, wave_x):
    freq_y, modul_y = frequency(wave_y)
    freq_z, modul_z = frequency(wave_z)
    freq_x, modul_x = frequency(wave_x)
    wave_square = (
        jnp.square(freq_x)[None, None, :]
        + jnp.square(freq_y)[:, None, None]
        + jnp.square(freq_z)[None, :, None]
    )
    positive = wave_square > 0.0
    gaussian = jnp.exp(-(math.pi * math.pi / (EWALD * EWALD)) * wave_square)
    kernel = jnp.where(positive, gaussian / jnp.where(positive, wave_square, 1.0), 0.0)
    moduli = modul_x[None, None, :] * modul_y[:, None, None] * modul_z[None, :, None]
    return kernel * moduli * (COULOMB / (math.pi * MESH**3))


def phases(left, right):
    turns = left[:, None] * right[None, :] % MESH
    angle = turns.astype(jnp.float32) * (2.0 * math.pi / MESH)
    return (jnp.cos(angle), jnp.sin(angle))


AXES = ("gx", "gy", "gz")


def source_of(coord):
    return 1 if coord == 0 else 0 if coord == 3 else coord - 1


def layer_kernel(
    ids, links, feats, geo, own, own_geo, radial_in, radial_out, mix_weight, out, s_acc, v_acc
):
    step = pl.program_id(0)
    atom_count = own.shape[0]

    @pl.when(step == 0)
    def _():
        s_acc[...] = jnp.zeros_like(s_acc)
        v_acc[...] = jnp.zeros_like(v_acc)

    picked = (links[...] == ids[...]).astype(jnp.float32).astype(jnp.bfloat16)
    rows = jnp.dot(picked, feats[...], preferred_element_type=jnp.float32)
    spots = jnp.dot(picked, geo[...], preferred_element_type=jnp.float32)
    edges = rows.shape[0]
    slots = edges // atom_count
    here = own_geo[...].astype(jnp.float32)
    located = jnp.concatenate([here[:, 0:3] + here[:, 3:6]] * slots, axis=0)
    displace = spots[:, 0:3] + spots[:, 3:6] - located
    length_sq = jnp.sum(displace * displace, axis=1, keepdims=True)
    distance = jnp.sqrt(length_sq)
    direction = displace / jnp.sqrt(length_sq + 1.0)
    spacing = ENV / (NB - 1)
    centres = lax.broadcasted_iota(jnp.int32, (edges, C), 1).astype(jnp.float32) * spacing
    envelope = jnp.square(jnp.maximum(1.0 - length_sq / (ENV * ENV), 0.0))
    basis = jnp.exp(-jnp.square((distance - centres) / spacing)) * envelope
    hidden = jnp.dot(
        basis.astype(jnp.bfloat16), radial_in[...], preferred_element_type=jnp.float32
    )
    hidden = (hidden / (1.0 + jnp.exp(-hidden))).astype(jnp.bfloat16)
    radial = jnp.dot(hidden, radial_out[...], preferred_element_type=jnp.float32)
    scalars = rows[:, :C]
    units = [direction[:, d : d + 1] for d in range(3)]
    vectors = [rows[:, C * (d + 1) : C * (d + 2)] for d in range(3)]
    projected = units[0] * vectors[0] + units[1] * vectors[1] + units[2] * vectors[2]
    scaled = radial[:, 2 * C : 3 * C] * scalars
    fourth = radial[:, 3 * C :]

    def over_slots(edge_values):
        return sum(edge_values[k * atom_count : (k + 1) * atom_count] for k in range(slots))

    s_acc[...] += over_slots(radial[:, :C] * scalars + radial[:, C : 2 * C] * projected)
    for d in range(3):
        v_acc[d] += over_slots(units[d] * scaled + fourth * vectors[d])

    @pl.when(step == pl.num_programs(0) - 1)
    def _():
        inverse_root = 1.0 / math.sqrt(NEIGH)
        previous = own[...].astype(jnp.float32)
        message = (s_acc[...] * inverse_root).astype(jnp.bfloat16)
        mixed = jnp.dot(message, mix_weight[0], preferred_element_type=jnp.float32)
        out[:, :C] = (previous[:, :C] + mixed / (1.0 + jnp.exp(-mixed))).astype(jnp.bfloat16)
        for d in range(3):
            message = (v_acc[d] * inverse_root).astype(jnp.bfloat16)
            mixed = jnp.dot(message, mix_weight[1], preferred_element_type=jnp.float32)
            span = slice(C * (d + 1), C * (d + 2))
            out[:, span] = (previous[:, span] + mixed).astype(jnp.bfloat16)


def layer(ids, links, feats, geo, own, own_geo, radial_in, radial_out, mix_weight):
    atom_count = own.shape[0]
    edge_block = 4 * atom_count
    whole = lambda array: pl.BlockSpec(array.shape, lambda i: (0,) * array.ndim)
    return pl.pallas_call(
        layer_kernel,
        grid=(links.shape[0] // edge_block,),
        out_shape=jax.ShapeDtypeStruct(own.shape, jnp.bfloat16),
        in_specs=[
            whole(ids),
            pl.BlockSpec((edge_block, 1), lambda i: (i, 0)),
            whole(feats),
            whole(geo),
            whole(own),
            whole(own_geo),
            whole(radial_in),
            whole(radial_out),
            whole(mix_weight),
        ],
        out_specs=pl.BlockSpec(own.shape, lambda i: (0, 0)),
        scratch_shapes=[
            pltpu.VMEM((atom_count, C), jnp.float32),
            pltpu.VMEM((3, atom_count, C), jnp.float32),
        ],
        compiler_params=pltpu.CompilerParams(
            dimension_semantics=("arbitrary",), vmem_limit_bytes=40 * 1024 * 1024
        ),
    )(ids, links, feats, geo, own, own_geo, radial_in, radial_out, mix_weight)


def ghost_plan(counts):
    groups = {}
    for number, corner in enumerate(outer_cells()):
        offset = tuple(offset_of(coord) for coord in corner)
        bits = [source_of(coord) for coord in corner]
        octant = 4 * bits[0] + 2 * bits[1] + bits[2]
        key = tuple(o % n for o, n in zip(offset, counts))
        groups.setdefault(key, []).append((number, octant, offset))
    return groups


def exchange(buffers, counts, groups):
    pieces = []
    devices = list(np.ndindex(*counts))
    linear = lambda spot: (spot[0] * counts[1] + spot[1]) * counts[2] + spot[2]
    for key, members in groups.items():
        octants = [member[1] for member in members]
        if octants == list(range(8)):
            block = buffers
        else:
            block = jnp.concatenate([buffers[o : o + 1] for o in octants], axis=0)
        if any(key):
            route = []
            for spot in devices:
                source = tuple((a + o) % n for a, o, n in zip(spot, key, counts))
                route.append((linear(source), linear(spot)))
            block = lax.ppermute(block, AXES, route)
        pieces.append(block)
    return jnp.concatenate(pieces, axis=0)


def shifted(block, axes, count, step):
    return lax.ppermute(block, axes, [((i + step) % count, i) for i in range(count)])


def gather_from(block, axes):
    count, me = lax.axis_size(axes), lax.axis_index(axes)
    pieces = [block] + [shifted(block, axes, count, step) for step in range(1, count)]
    return lax.dynamic_slice_in_dim(jnp.stack(pieces + pieces), count - me, count, 0)


def sum_to(blocks, axes):
    count, me = lax.axis_size(axes), lax.axis_index(axes)
    turned = lax.dynamic_slice_in_dim(jnp.concatenate([blocks, blocks]), me, count, 0)
    return turned[0] + sum(
        shifted(turned[step], axes, count, count - step) for step in range(1, count)
    )


def cas_table(left, right):
    cosine, sine = phases(left, right)
    return cosine + sine


def local_rows(coefficient, first, span):
    slot_index = jnp.arange(span, dtype=jnp.int32)[None, :, None]
    summed = 0.0
    for offset in range(4):
        summed = summed + jnp.where(
            slot_index == ((first + offset) % MESH)[:, None, :], coefficient[offset][:, None, :], 0.0
        )
    return summed


def mm(pattern, left, right):
    return jnp.einsum(
        pattern, left, right, precision=lax.Precision.HIGH, preferred_element_type=jnp.float32
    )


def per_device(
    features,
    fraction,
    cell_index,
    species,
    octant_rows,
    neighbours,
    radial_in,
    radial_out,
    mix_weight,
    readout,
    species_table,
):
    bf16 = jnp.bfloat16
    current = features[0, 0, 0]
    fraction_here = fraction[0, 0, 0]
    cells_here = cell_index[0, 0, 0]
    kinds = species[0, 0, 0]
    chosen_rows = octant_rows[0, 0, 0].reshape(-1)
    links = neighbours[0, 0, 0].reshape(-1, 1)
    atom_count, feat_width = current.shape
    ghost_count = chosen_rows.shape[0] // 8
    counts = tuple(lax.axis_size(axis) for axis in AXES)
    count_x, count_y, count_z = counts
    total = count_x * count_y * count_z
    span_x, span_y, span_z = (MESH // n for n in counts)
    small = jnp.concatenate([cells_here.astype(bf16), fraction_here], axis=0)
    own_geo = jnp.pad(jnp.transpose(small), ((0, 0), (0, C - 6)))
    pick = (chosen_rows[:, None] == jnp.arange(atom_count, dtype=jnp.int32)[None, :]).astype(bf16)
    groups = ghost_plan(counts)
    ids = list(range(atom_count))
    shift_rows = []
    for members in groups.values():
        for number, _, offset in members:
            ids += [atom_count + number * ghost_count + r for r in range(ghost_count)]
            shift = [o * w for o, w in zip(offset, (span_x, span_y, span_z))]
            shift_rows += [shift] * ghost_count
    real_rows = len(ids)
    table_rows = -(-real_rows // 128) * 128
    ids = jnp.asarray(np.array(ids + [-1] * (table_rows - real_rows), np.int32))[None, :]
    shift_rows = np.pad(np.array(shift_rows, np.float32), ((0, 0), (0, C - 3)))
    fill = table_rows - real_rows

    def outgoing(values):
        return jnp.dot(pick, values, preferred_element_type=jnp.float32).astype(bf16).reshape(
            8, ghost_count, -1
        )

    geo = own_geo
    for index in range(LAYERS):
        values = jnp.concatenate([current, own_geo], axis=1) if index == 0 else current
        arrived = exchange(outgoing(values), counts, groups).reshape(
            real_rows - atom_count, values.shape[1]
        )
        feats = jnp.concatenate(
            [current, arrived[:, :feat_width], jnp.zeros((fill, feat_width), bf16)], axis=0
        )
        if index == 0:
            ghost_geo = (arrived[:, feat_width:].astype(jnp.float32) + shift_rows).astype(bf16)
            geo = jnp.concatenate([own_geo, ghost_geo, jnp.zeros((fill, C), bf16)], axis=0)
        first_pad = jnp.pad(radial_in[index], ((0, C - NB), (0, C - radial_in.shape[2])))
        second_pad = jnp.pad(radial_out[index], ((0, C - radial_out.shape[1]), (0, 0)))
        current = layer(
            ids, links, feats, geo, current, own_geo, first_pad, second_pad, mix_weight[index]
        )

    head_out = jnp.dot(current[:, :C], readout, preferred_element_type=jnp.float32)
    one_hot = (
        kinds[:, None] == jnp.arange(species_table.shape[0], dtype=jnp.int32)[None, :]
    ).astype(jnp.float32)
    species_term = jnp.dot(
        one_hot, species_table, precision=HIGHEST_PRECISION, preferred_element_type=jnp.float32
    )
    base_energy = head_out[:, 0] + species_term[:, 0]
    charge = head_out[:, 1] + species_term[:, 1]
    packed = jnp.concatenate([charge[None], small.astype(jnp.float32)], axis=0)
    packed = gather_from(gather_from(packed, ("gy", "gz")), ("gx",))
    charges = packed[:, :, 0].reshape(count_x, -1)
    everyone = packed[:, :, 1:]

    device = (lax.axis_index("gx") * count_y + lax.axis_index("gy")) * count_z
    device = device + lax.axis_index("gz")
    wave_count = MESH // total
    waves_y = device * wave_count + jnp.arange(wave_count, dtype=jnp.int32)
    full = jnp.arange(MESH, dtype=jnp.int32)
    table = everyone.reshape(count_x, count_y * count_z, 6, atom_count)
    table = jnp.transpose(table, (2, 0, 1, 3)).reshape(6, count_x, -1).astype(jnp.float32)
    all_cells = table[:3].astype(jnp.int32)
    weights, slopes = spline(table[3:])
    order = jnp.arange(count_y * count_z * atom_count, dtype=jnp.int32) // atom_count
    start_y = (order // count_z * span_y)[None, :]
    start_z = (order % count_z * span_z)[None, :]
    width_x = -(-(span_x + 3) // 8) * 8
    weight_x = local_rows(weights[:, 0], all_cells[0], width_x)
    slope_x = local_rows(slopes[:, 0], all_cells[0], width_x)
    first_z = all_cells[2] + start_z + (MESH - 1)
    weight_z = local_rows(weights[:, 2], first_z, MESH)
    slope_z = local_rows(slopes[:, 2], first_z, MESH)
    place_y = all_cells[1] + start_y
    turns = (waves_y[:, None, None] * place_y[None]) % MESH
    angle = turns.astype(jnp.float32) * (2.0 * math.pi / MESH)
    cosine_y, sine_y = jnp.cos(angle), jnp.sin(angle)
    step_cosine, step_sine = phases(waves_y, jnp.arange(4, dtype=jnp.int32) - 1 + MESH)
    plus, minus = step_cosine + step_sine, step_cosine - step_sine

    def along_y(values):
        first = sum(plus[:, m][:, None, None] * values[m][None] for m in range(4))
        second = sum(minus[:, m][:, None, None] * values[m][None] for m in range(4))
        return cosine_y * first + sine_y * second

    weight_y = along_y(weights[:, 1])
    slope_y = along_y(slopes[:, 1])
    slots_x = (
        jnp.arange(count_x, dtype=jnp.int32)[:, None] * span_x
        + jnp.arange(width_x, dtype=jnp.int32)[None, :]
        + (MESH - 1)
    ).reshape(-1) % MESH
    cas_x = cas_table(full, slots_x).reshape(MESH, count_x, width_x)
    cas_z = cas_table(full, full)
    influence_here = influence(waves_y, full, full)

    loaded = (jnp.transpose(weight_y, (1, 0, 2)) * charges[:, None, :])[:, :, None, :]
    loaded = loaded * weight_x[:, None, :, :]
    spread = mm("ikxa,iza->ikxz", loaded, weight_z)
    spectrum = mm("ikxz,zw->ikxw", spread, cas_z)
    spectrum = mm("vix,ikxw->kwv", cas_x, spectrum) * influence_here
    back = mm("vix,kwv->ikxw", cas_x, spectrum)
    back = mm("ikxw,wz->ikxz", back, cas_z)
    level = mm("ikxz,iza->ikxa", back, weight_z)
    level_slope = mm("ikxz,iza->ikxa", back, slope_z)
    by_x = jnp.transpose(jnp.sum(level * weight_x[:, None], axis=2), (1, 0, 2))
    by_slope_x = jnp.transpose(jnp.sum(level * slope_x[:, None], axis=2), (1, 0, 2))
    by_slope_z = jnp.transpose(jnp.sum(level_slope * weight_x[:, None], axis=2), (1, 0, 2))
    partial = jnp.stack(
        [
            jnp.sum(weight_y * by_x, axis=0),
            jnp.sum(weight_y * by_slope_x, axis=0),
            jnp.sum(slope_y * by_x, axis=0),
            jnp.sum(weight_y * by_slope_z, axis=0),
        ]
    )
    partial = jnp.transpose(
        partial.reshape(4, count_x, count_y * count_z, atom_count), (1, 2, 0, 3)
    )
    mine = sum_to(sum_to(partial, ("gx",)), ("gy", "gz"))
    recip_force = -charge[None, :] * mine[1:]
    site_energy = base_energy + 0.5 * charge * mine[0]
    return (current[None, None, None], site_energy[None, None, None], recip_force[None, None, None])


def solution(mesh):
    in_specs = (
        P("gx", "gy", "gz", None, None),
        P("gx", "gy", "gz", None, None),
        P("gx", "gy", "gz", None, None),
        P("gx", "gy", "gz", None),
        P("gx", "gy", "gz", None, None),
        P("gx", "gy", "gz", None, None),
        P(),
        P(),
        P(),
        P(),
        P(),
    )
    out_specs = (
        P("gx", "gy", "gz", None, None),
        P("gx", "gy", "gz", None),
        P("gx", "gy", "gz", None, None),
    )
    return jax.shard_map(
        per_device, mesh=mesh, in_specs=in_specs, out_specs=out_specs, check_vma=False
    )
```
